32 devices in a mesh: group: 1, node: 8 (over z, core), dev: 4 (over y, x).
Axes of the slice: x: 2, y: 2, z: 4, core: 2. Of those that a mesh axis runs over, the one named last changes fastest.
Arguments:
- tokens: bfloat16 [4096, 2048], P(('group', 'node', 'dev')), may hold values from -6 to 6
- node_choice: int32 [4096, 4], P(('group', 'node', 'dev')), may hold values from 0 to 7, all different within a row; in each aligned block of 128 rows (0 to 127, 128 to 255, ...) at most 96 rows name the same one
- local_pick: int32 [4096, 4, 2], P(('group', 'node', 'dev')), may hold values from 0 to 3, all different within a row
- gate_scores: float32 [4096, 32], P(('group', 'node', 'dev')), may hold values from 0.1 to 2
- placement: int32 [32], replicated, may hold values from 0 to 31, as said below
- w_gate: bfloat16 [32, 2048, 768], P(('node', 'dev')), may hold values from -0.125 to 0.125
- w_up: bfloat16 [32, 2048, 768], P(('node', 'dev')), may hold values from -0.125 to 0.125
- w_down: bfloat16 [32, 768, 2048], P(('node', 'dev')), may hold values from -0.21875 to 0.21875
Outputs:
- mixed: bfloat16 [4096, 2048], P(('group', 'node', 'dev'))
The draws below stay inside these ranges and needn't reach their ends.
Inputs may be any that keep to these rules, and one draw needn't show every extreme that they name: `placement`: the 4 experts g * 4 to g * 4 + 3 of group g sit on the 4 devices of one node, one expert a device; each device holds one expert. `node_choice`: each token names 4 different groups; among the tokens of one device no group is named by more than 96, a bound that some block reaches. `local_pick`: the 2 members taken in one group are different.
All inputs are finite; a program needn't handle non-finite values.
Results may differ from the reference program's by a relative error of at most 0.0085.
Values may be sent and summed in bfloat16 or wider, within the bound.
A program may use at most 128 MiB of HBM per device.

```python
import math
import jax
import jax.numpy as jnp
import numpy as np
from jax import lax

D = 2048
FF = 768
TOK_DEV = 128
NODE_PICK = 4
PAIR = 2
EXPERTS = 32
TOKENS = 4096
MOST = 96
N_NODE = 8
N_DEV = 4


def draw_placement(key, part):
    key = jax.random.fold_in(key, 7)
    node_key, dev_key = jax.random.split(key)
    node_order = jax.random.permutation(node_key, N_NODE)
    dev_keys = jax.random.split(dev_key, N_NODE)
    dev_order = jax.vmap(lambda k: jax.random.permutation(k, N_DEV))(dev_keys)
    return (node_order[:, None] * N_DEV + dev_order).reshape(-1).astype(jnp.int32)


def steps_of(key, dims, shards, smallest, top_value):
    def one(axis_at, shards_of):
        draws = jax.random.uniform(jax.random.fold_in(jax.random.fold_in(key, 6), axis_at), (shards_of,), jnp.float32, smallest / len(shards), top_value / len(shards))
        return jnp.repeat(jnp.exp(draws), dims[axis_at] // shards_of).reshape((-1,) + (1,) * (len(dims) - axis_at - 1))

    loudness = one(*shards[0])
    for cut in shards[1:]:
        loudness = loudness * one(*cut)
    return loudness


def picks_of(stream_key, rows, number_of, top, lift):
    order = jax.random.permutation(jax.random.fold_in(stream_key, 1), number_of)
    favour = order
    for power in range(3):
        favour = favour * favour // number_of
    favour = favour * lift // number_of
    chance = jax.random.randint(jax.random.fold_in(stream_key, 2), (rows, number_of), 0, 4096) + favour
    fixed_rows = jax.random.permutation(jax.random.fold_in(stream_key, 3), rows)[jnp.arange(number_of) % rows]
    chance = jnp.where(jnp.arange(rows)[:, None] == fixed_rows[None, :], 1 << 14, chance)
    score = chance * number_of + jnp.arange(number_of)
    return lax.top_k(score.astype(jnp.int32), top)[1].astype(jnp.int32)


def routed_block(own_key, own, number, rows, count, top, reach, lean):
    ranking = jax.random.permutation(own_key, count)
    heavy_load, ordinary = load_shares(count, rows * top, reach, lean, True), load_shares(count, rows * top, reach, lean, False)
    places = jnp.arange(count)

    def named(sizes, offset_by):
        used = int((sizes > 0).sum())
        fixed = max(1, used // 4)
        passed = fixed + (places - fixed + offset_by * (used - fixed)) % max(1, count - fixed)
        return jnp.zeros((count,), jnp.int32).at[ranking[jnp.where(places < fixed, places, passed)]].set(jnp.asarray(sizes, jnp.int32))

    sizes = jnp.where(number % 4 == 0, named(heavy_load, number // 4), named(ordinary, number - number // 4 - 1))
    mixed = jax.random.permutation(jax.random.fold_in(own, 3), count)
    giver, sink = mixed[0:count // 2 * 2:2], mixed[1:count // 2 * 2:2]
    room = jnp.minimum(sizes[giver] - 1, reach - sizes[sink]) // 2
    room = jnp.where((giver == ranking[0]) | (sink == ranking[0]) | (sizes[sink] == 0), 0, jnp.maximum(room, 0))
    passed = jax.random.randint(jax.random.fold_in(own, 4), (count // 2,), 0, 1 << 20) % (room + 1)
    sizes = sizes.at[giver].add(-passed).at[sink].add(passed)
    items = jnp.searchsorted(jnp.cumsum(sizes), jnp.arange(rows * top), side="right").astype(jnp.int32)
    listing = items.reshape(top, rows).T
    listing = listing[jax.random.permutation(jax.random.fold_in(own, 1), rows)]
    offset_by = jax.random.randint(jax.random.fold_in(own, 2), (rows, 1), 0, top)
    return jnp.take_along_axis(listing, (jnp.arange(top)[None, :] + offset_by) % top, axis=1)


def load_shares(number_of, total, most, slope, full):
    portions = [(1 << 20) // math.isqrt(grade ** slope) + 1 for grade in range(1, number_of + 1)]
    largest = most if full else min(most, max(-(-total // number_of), total * portions[0] // sum(portions)))
    least = 1 if total - largest >= number_of - 1 else 0
    counts, spare = [largest] + [least] * (number_of - 1), total - largest - least * (number_of - 1)
    while spare > 0:
        movable = [i for i in range(1, number_of) if counts[i] < largest] or [i for i in range(1, number_of) if counts[i] < most]
        pool, remaining = sum([portions[i] for i in movable]), spare
        for i in movable:
            more = min(most - counts[i], max(1, remaining * portions[i] // pool), spare)
            counts[i] = counts[i] + more
            spare = spare - more
    return np.array(counts)


def bell_draw(stream_key, dims, width, bound, pieces=(), held_as=jnp.bfloat16):
    gain = steps_of(stream_key, dims, pieces, -0.22, 0.18) if pieces else 1.0
    drawn = jax.random.normal(stream_key, dims, jnp.float32) * width * gain
    return jnp.minimum(jnp.maximum(drawn, -bound), bound).astype(held_as)


def setup_inputs(seed: int = 0, part: int = 0) -> dict:
    arg_keys = jax.random.split(jax.random.key(seed), 9)
    own_keys = jax.random.split(jax.random.fold_in(arg_keys[8], part), 9)
    tokens = bell_draw(own_keys[0], (TOKENS, D), 1.0, 6.0, ((0, 32),))
    node_choice_keys = jax.random.split(jax.random.fold_in(own_keys[1], 1), TOKENS // TOK_DEV)
    node_choice_turns = jax.random.permutation(jax.random.fold_in(own_keys[1], 3), TOKENS // TOK_DEV)
    node_choice = jax.vmap(lambda own, number: routed_block(jax.random.fold_in(own_keys[1], 2), own, number, TOK_DEV, N_NODE, NODE_PICK, MOST, 1))(node_choice_keys, node_choice_turns).reshape((TOKENS, NODE_PICK))
    local_pick = picks_of(own_keys[2], TOKENS * NODE_PICK, N_DEV, PAIR, 0).reshape((TOKENS, NODE_PICK, PAIR))
    gate_scores = jnp.clip(jnp.exp(math.log(2.0) - 2.9957323 * jax.random.uniform(own_keys[3], (TOKENS, EXPERTS), jnp.float32) ** steps_of(own_keys[3], (TOKENS, EXPERTS), ((0, 32),), -0.2, 0.2)), 0.1, 2.0)
    placement = draw_placement(jax.random.fold_in(arg_keys[8], 71), part)
    w_gate = bell_draw(arg_keys[5], (EXPERTS, D, FF), D ** -0.5, 0.125, ((0, 32),))
    w_up = bell_draw(arg_keys[6], (EXPERTS, D, FF), D ** -0.5, 0.125, ((0, 32),))
    w_down = bell_draw(arg_keys[7], (EXPERTS, FF, D), FF ** -0.5, 0.21875, ((0, 32),))
    return dict(tokens=tokens, node_choice=node_choice, local_pick=local_pick, gate_scores=gate_scores, placement=placement, w_gate=w_gate, w_up=w_up, w_down=w_down)


def reference(tokens, node_choice, local_pick, gate_scores, placement, w_gate, w_up, w_down):
    per_token = NODE_PICK * PAIR
    pair_total = TOKENS * per_token
    expert_ids = (node_choice[:, :, None] * N_DEV + local_pick).reshape(TOKENS, per_token).astype(jnp.int32)
    slot_ids = placement[expert_ids].reshape(-1).astype(jnp.int32)
    raw_scores = jnp.take_along_axis(gate_scores, expert_ids, axis=1)
    gate_values = (raw_scores / jnp.sum(raw_scores, axis=1, keepdims=True)).astype(jnp.bfloat16).reshape(-1)
    pair_order = jnp.argsort(slot_ids, stable=True).astype(jnp.int32)
    slot_counts = jnp.zeros((EXPERTS,), jnp.int32).at[slot_ids].add(jnp.ones((pair_total,), jnp.int32))
    offsets = (jnp.cumsum(slot_counts) - slot_counts).astype(jnp.int32)
    block_rows = 512
    order_padded = jnp.concatenate([pair_order, jnp.full((block_rows,), pair_total, jnp.int32)])
    terms = jnp.zeros((pair_total, D), jnp.bfloat16)

    def per_expert(slot_index, terms):
        slot_index = jnp.asarray(slot_index).astype(jnp.int32)
        gate_matrix = w_gate[slot_index]
        up_matrix = w_up[slot_index]
        down_matrix = w_down[slot_index]
        slot_count = slot_counts[slot_index]

        def per_block(block_index, terms):
            block_start = (jnp.asarray(block_index) * block_rows).astype(jnp.int32)
            first_row = (offsets[slot_index] + block_start).astype(jnp.int32)
            pair_index = lax.dynamic_slice_in_dim(order_padded, first_row, block_rows).astype(jnp.int32)
            in_range = (block_start + jnp.arange(block_rows, dtype=jnp.int32)) < slot_count
            pair_index = jnp.where(in_range, pair_index, pair_total).astype(jnp.int32)
            clamped = jnp.minimum(pair_index, pair_total - 1).astype(jnp.int32)
            row_block = tokens[clamped // per_token]
            gate_part = jnp.dot(row_block, gate_matrix, preferred_element_type=jnp.float32)
            up_part = jnp.dot(row_block, up_matrix, preferred_element_type=jnp.float32)
            hidden = (jax.nn.silu(gate_part) * up_part).astype(jnp.bfloat16)
            result = jnp.dot(hidden, down_matrix, preferred_element_type=jnp.float32).astype(jnp.bfloat16)
            weighted = (gate_values[clamped].astype(jnp.float32)[:, None] * result.astype(jnp.float32)).astype(jnp.bfloat16)
            return terms.at[pair_index].set(weighted, mode="drop")

        block_count = ((slot_count + block_rows - 1) // block_rows).astype(jnp.int32)
        return lax.fori_loop(jnp.int32(0), block_count, per_block, terms)

    terms = lax.fori_loop(0, EXPERTS, per_expert, terms)
    terms = terms.reshape(TOKENS, NODE_PICK, PAIR, D)
    node_part = jnp.sum(terms.astype(jnp.float32), axis=2).astype(jnp.bfloat16)
    return jnp.sum(node_part.astype(jnp.float32), axis=1).astype(jnp.bfloat16)
```

```python
import functools

import jax
import jax.numpy as jnp
from jax import lax
from jax.experimental import pallas as pl
from jax.experimental.pallas import tpu as pltpu
from jax.sharding import PartitionSpec as P

MESH = pl.DeviceIdType.MESH
ROWS = 16


def expert_terms(slot_rows, slot_gates, gate_matrix, up_matrix, down_matrix):
    row_total = slot_rows.shape[0]
    width = slot_rows.shape[1]
    live_mask = slot_gates > 0
    live_int = live_mask.astype(jnp.int32)
    live_count = jnp.sum(live_int)
    live_before = jnp.cumsum(live_int) - live_int
    spare_before = jnp.arange(row_total, dtype=jnp.int32) - live_before
    position = jnp.where(live_mask, live_before, live_count + spare_before)
    block_rows = min(512, row_total)
    padded_rows = -(-row_total // block_rows) * block_rows
    packed = jnp.zeros((padded_rows, width), jnp.bfloat16).at[position].set(slot_rows)
    outputs = jnp.zeros((padded_rows, down_matrix.shape[1]), jnp.bfloat16)

    def one_block(block_index, outputs):
        first_row = block_index * block_rows
        row_block = lax.dynamic_slice_in_dim(packed, first_row, block_rows, 0)
        gate_part = jnp.dot(row_block, gate_matrix, preferred_element_type=jnp.float32)
        up_part = jnp.dot(row_block, up_matrix, preferred_element_type=jnp.float32)
        hidden = (jax.nn.silu(gate_part) * up_part).astype(jnp.bfloat16)
        result = jnp.dot(hidden, down_matrix, preferred_element_type=jnp.float32).astype(
            jnp.bfloat16
        )
        return lax.dynamic_update_slice_in_dim(outputs, result, first_row, 0)

    block_count = (live_count + block_rows - 1) // block_rows
    outputs = lax.fori_loop(0, block_count, one_block, outputs)
    restored = outputs[position]
    return (slot_gates.astype(jnp.float32)[:, None] * restored.astype(jnp.float32)).astype(
        jnp.bfloat16
    )


def arrival_ranks(targets, target_count):
    onehot = (targets[:, None] == jnp.arange(target_count, dtype=jnp.int32)).astype(jnp.int32)
    return jnp.sum(jnp.cumsum(onehot, axis=0) * onehot, axis=-1) - 1


def local(tokens, node_choice, local_pick, gate_scores, placement, w_gate, w_up, w_down):
    tok_count = tokens.shape[0]
    width = tokens.shape[1]
    groups_each = node_choice.shape[1]
    pair_each = local_pick.shape[2]
    node_count = lax.axis_size("node")
    dev_count = lax.axis_size("dev")
    expert_total = placement.shape[0]
    capacity = min(tok_count, max(2, 3 * tok_count * groups_each // (2 * node_count)))
    gate_matrix = w_gate[0]
    up_matrix = w_up[0]
    down_matrix = w_down[0]
    expert_ids = node_choice[:, :, None] * dev_count + local_pick
    matches = expert_ids[..., None] == jnp.arange(expert_total, dtype=jnp.int32)
    slot_ids = jnp.sum(jnp.where(matches, placement, 0), axis=-1)
    raw_scores = jnp.sum(jnp.where(matches, gate_scores[:, None, None, :], 0.0), axis=-1)
    gate_values = (raw_scores / jnp.sum(raw_scores, axis=(1, 2), keepdims=True)).astype(
        jnp.bfloat16
    )
    flat_slots = slot_ids.reshape(-1)
    slot_ranks = arrival_ranks(flat_slots, expert_total)
    target = flat_slots * capacity + slot_ranks
    pair_rows = jnp.broadcast_to(
        tokens[:, None, None, :], (tok_count, groups_each, pair_each, width)
    ).reshape(-1, width)
    send_rows = jnp.zeros((expert_total * capacity, width), jnp.bfloat16).at[target].set(pair_rows)
    send_gates = (
        jnp.zeros((expert_total * capacity,), jnp.bfloat16).at[target].set(gate_values.reshape(-1))
    )
    recv_rows, recv_gates = (
        lax.all_to_all(
            send_rows.reshape(expert_total, capacity, width),
            ("node", "dev"),
            split_axis=0,
            concat_axis=0,
            tiled=True,
        ),
        lax.all_to_all(
            send_gates.reshape(expert_total, capacity),
            ("node", "dev"),
            split_axis=0,
            concat_axis=0,
            tiled=True,
        ),
    )
    weighted = expert_terms(
        recv_rows.reshape(-1, width), recv_gates.reshape(-1), gate_matrix, up_matrix, down_matrix
    )
    returned = lax.all_to_all(
        weighted.reshape(expert_total, capacity, width),
        ("node", "dev"),
        split_axis=0,
        concat_axis=0,
        tiled=True,
    )
    pair_terms = returned.reshape(-1, width)[target].reshape(
        tok_count, groups_each, pair_each, width
    )
    node_part = jnp.sum(pair_terms.astype(jnp.float32), axis=2).astype(jnp.bfloat16)
    return jnp.sum(node_part.astype(jnp.float32), axis=1).astype(jnp.bfloat16)


def fused_kernel(layers, tok_ref, node_ref, pick_ref, score_ref, place_ref, wg_hbm, wu_hbm, wd_hbm,
                 out_ref, held, spare, from_core, half_x, half_y, whole_x, whole_y, rise, fall,
                 wg, wu, wd, hid, core_s, core_r, back_s, back_r, ax_s, ax_r, load_s):
    tok, width = tok_ref.shape
    half = tok // 2
    n = lax.axis_index("node")
    d = lax.axis_index("dev")
    z, k = n // 2, n % 2
    x, y = d % 2, d // 2
    dx = y * 2 + (1 - x)
    dy = (1 - y) * 2 + x
    dd = (1 - y) * 2 + (1 - x)
    mate = {"node": z * 2 + 1 - k, "dev": d}
    to_x = {"node": n, "dev": dx}
    to_y = {"node": n, "dev": dy}
    up = {"node": n + 2, "dev": d}
    down = {"node": n - 2, "dev": d}
    has_up, has_down = z < layers - 1, z > 0
    middle = ((z + 1) // 2) % 2

    def near(j):
        j = j + middle * (j // 2) * (5 - 2 * j)
        return ((z // 2 + j // 2) % 2) * 2 + (z + j) % 2

    loads = [
        pltpu.make_async_copy(src.at[0], dst, load_s.at[i])
        for i, (src, dst) in enumerate(((wg_hbm, wg), (wu_hbm, wu), (wd_hbm, wd)))
    ]
    for load in loads:
        load.start()

    experts = score_ref.shape[1]
    lane = lax.broadcasted_iota(jnp.int32, (tok, experts), 1)
    hit = jnp.zeros((tok, experts), jnp.float32)
    groups, pair = node_ref.shape[1], pick_ref.shape[1] // node_ref.shape[1]
    for g in range(groups):
        for p in range(pair):
            c = g * pair + p
            expert = node_ref[:, g : g + 1] * 4 + pick_ref[:, c : c + 1]
            hit = jnp.where(lane == expert, 1.0, hit)
    raw = hit * score_ref[...]
    gates = (raw / jnp.sum(raw, axis=1, keepdims=True)).astype(jnp.bfloat16)
    mine = z * 4 + d
    held[mine, 0, :, pl.ds(0, width)] = tok_ref[...]
    held[mine, 0, :, pl.ds(width, 128)] = jnp.concatenate(
        [gates, jnp.zeros((tok, 128 - experts), jnp.bfloat16)], axis=1
    )

    barrier = pltpu.get_barrier_semaphore()
    for other in (mate, to_x, to_y):
        pl.semaphore_signal(barrier, inc=1, device_id=other, device_id_type=MESH)

    @pl.when(has_up)
    def _():
        pl.semaphore_signal(barrier, inc=1, device_id=up, device_id_type=MESH)

    @pl.when(has_down)
    def _():
        pl.semaphore_signal(barrier, inc=1, device_id=down, device_id_type=MESH)

    pl.semaphore_wait(barrier, 4 + middle)

    def remote(src, dst, send, recv, to):
        return pltpu.make_async_remote_copy(
            src_ref=src, dst_ref=dst, send_sem=send, recv_sem=recv, device_id=to,
            device_id_type=MESH,
        )

    def along(kind, zp, src, dst, to):
        return remote(src, dst, ax_s.at[kind, zp], ax_r.at[kind, zp], to)

    lo, hi = pl.ds(0, half), pl.ds(half, half)
    cols = pl.ds(0, width)

    def g_up(zp):
        return along(0, zp, held.at[zp * 4 + d, 0], held.at[zp * 4 + d, 0], up)

    def g_down(zp):
        return along(1, zp, held.at[zp * 4 + d, 0], held.at[zp * 4 + d, 0], down)

    def g_x(zp, dev):
        return along(2, zp, held.at[zp * 4 + dev, 0], held.at[zp * 4 + dev, 0], to_x)

    def g_y(zp, dev):
        return along(3, zp, held.at[zp * 4 + dev, 0], held.at[zp * 4 + dev, 0], to_y)

    def g_xh(zp, dev):
        part = held.at[zp * 4 + dev, 0, hi]
        return along(4, zp, part, part, to_x)

    def g_yh(zp, dev):
        part = held.at[zp * 4 + dev, 0, lo]
        return along(5, zp, part, part, to_y)

    def g_core(chip):
        return remote(held.at[chip, 0], held.at[chip, 1], core_s.at[chip], core_r.at[chip], mate)

    def b_core(chip):
        return remote(spare.at[chip], from_core.at[chip], back_s.at[chip], back_r.at[chip], mate)

    def b_xh(zp):
        return along(6, zp, held.at[zp * 4 + dd, 1, lo, cols], half_x.at[zp], to_x)

    def b_yh(zp):
        return along(7, zp, held.at[zp * 4 + dd, 1, hi, cols], half_y.at[zp], to_y)

    def b_x(zp):
        return along(8, zp, held.at[zp * 4 + dx, 1, :, cols], whole_x.at[zp], to_x)

    def b_y(zp):
        return along(9, zp, held.at[zp * 4 + dy, 1, :, cols], whole_y.at[zp], to_y)

    def b_up(zp):
        return along(10, zp, held.at[zp * 4 + d, 1, :, cols], rise.at[zp], up)

    def b_down(zp):
        return along(11, zp, held.at[zp * 4 + d, 1, :, cols], fall.at[zp], down)

    mask = (place_ref[...] == n * 4 + d).astype(jnp.float32)

    def experts_of(chip):
        def first(i, _):
            at = pl.ds(pl.multiple_of(i * 256, 256), 256)
            rows = held[chip, :, :, cols].reshape(2 * tok, width)
            a = jnp.dot(rows, wg[:, at], preferred_element_type=jnp.float32)
            b = jnp.dot(rows, wu[:, at], preferred_element_type=jnp.float32)
            hid[:, at] = (a / (1.0 + jnp.exp(-a)) * b).astype(jnp.bfloat16)
            return 0

        lax.fori_loop(0, wg.shape[1] // 256, first, 0)
        weights = held[chip, :, :, pl.ds(width, 128)].reshape(2 * tok, 128).astype(jnp.float32)
        weight = jnp.sum(weights * mask, axis=1, keepdims=True)

        def second(i, _):
            at = pl.ds(pl.multiple_of(i * 256, 256), 256)
            got = jnp.dot(hid[...], wd[:, at], preferred_element_type=jnp.float32)
            term = (weight * got.astype(jnp.bfloat16).astype(jnp.float32)).astype(jnp.bfloat16)
            held[chip, 1, :, at] = term[:tok]
            spare[chip, :, at] = term[tok:]
            return 0

        lax.fori_loop(0, width // 256, second, 0)

    def gather_step(t, _):
        @pl.when(t < layers)
        def _():
            zp = near(t)

            @pl.when(zp < z)
            def _():
                g_up(zp).wait_recv()

            @pl.when(zp > z)
            def _():
                g_down(zp).wait_recv()

            @pl.when(jnp.logical_and(zp <= z, has_up))
            def _():
                g_up(zp).start()

            @pl.when(jnp.logical_and(zp >= z, has_down))
            def _():
                g_down(zp).start()

            g_x(zp, d).start()
            g_y(zp, d).start()
            g_core(zp * 4 + d).start()

        @pl.when(jnp.logical_and(t >= 1, t < layers + 1))
        def _():
            zp = near(t - 1)
            g_x(zp, dx).wait_recv()
            g_yh(zp, dx).start()
            g_core(zp * 4 + dx).start()
            g_y(zp, dy).wait_recv()
            g_xh(zp, dy).start()
            g_core(zp * 4 + dy).start()

        @pl.when(t >= 2)
        def _():
            zp = near(t - 2)
            g_xh(zp, dd).wait_recv()
            g_yh(zp, dd).wait_recv()
            g_core(zp * 4 + dd).start()

        @pl.when(t == 0)
        def _():
            for load in loads:
                load.wait()

        def work(c, _):
            j = t - (c + 1) // 2

            @pl.when(jnp.logical_and(j >= 0, j < layers))
            def _():
                cx, cy = (x + c) % 2, (y + c // 2) % 2
                chip = near(j) * 4 + cy * 2 + cx
                g_core(chip).wait_recv()
                experts_of(chip)
                b_core(chip).start()

            return 0

        lax.fori_loop(0, 4, work, 0)
        return 0

    lax.fori_loop(0, layers + 2, gather_step, 0)

    def total(chip, count, extra):
        def rows(i, _):
            at = pl.ds(pl.multiple_of(i * ROWS, ROWS), ROWS)
            value = held[chip, 1, at, cols].astype(jnp.float32)
            value = value + from_core[chip, at, :].astype(jnp.float32)
            for ref, zp in extra:
                value = value + ref[zp, at, :].astype(jnp.float32)
            held[chip, 1, at, cols] = value.astype(jnp.bfloat16)
            return 0

        lax.fori_loop(0, count // ROWS, rows, 0)

    def more(chip, first, count, ref, zp):
        def rows(i, _):
            at = pl.ds(pl.multiple_of(i * ROWS, ROWS), ROWS)
            to = pl.ds(pl.multiple_of(first + i * ROWS, ROWS), ROWS)
            value = held[chip, 1, to, cols].astype(jnp.float32) + ref[zp, at, :].astype(jnp.float32)
            held[chip, 1, to, cols] = value.astype(jnp.bfloat16)
            return 0

        lax.fori_loop(0, count // ROWS, rows, 0)

    def back_step(u, _):
        @pl.when(u < layers)
        def _():
            zp = near(layers - 1 - u)
            chip = zp * 4 + dd
            b_core(chip).wait_recv()
            total(chip, tok, ())
            b_xh(zp).start()
            b_yh(zp).start()

        @pl.when(jnp.logical_and(u >= 1, u < layers + 1))
        def _():
            zp = near(layers - u)
            b_core(zp * 4 + dx).wait_recv()
            total(zp * 4 + dx, tok, ())
            b_yh(zp).wait_recv()
            more(zp * 4 + dx, half, half, half_y, zp)
            b_x(zp).start()
            b_core(zp * 4 + dy).wait_recv()
            total(zp * 4 + dy, tok, ())
            b_xh(zp).wait_recv()
            more(zp * 4 + dy, 0, half, half_x, zp)
            b_y(zp).start()

        @pl.when(u >= 2)
        def _():
            zp = near(layers + 1 - u)
            chip = zp * 4 + d
            b_core(chip).wait_recv()
            b_x(zp).wait_recv()
            b_y(zp).wait_recv()
            total(chip, tok, ((whole_x, zp), (whole_y, zp)))

            @pl.when(jnp.logical_and(zp >= z, has_down))
            def _():
                b_up(zp).wait_recv()
                more(chip, 0, tok, rise, zp)

            @pl.when(jnp.logical_and(zp <= z, has_up))
            def _():
                b_down(zp).wait_recv()
                more(chip, 0, tok, fall, zp)

            @pl.when(zp > z)
            def _():
                b_up(zp).start()

            @pl.when(zp < z)
            def _():
                b_down(zp).start()

        return 0

    lax.fori_loop(0, layers + 2, back_step, 0)
    out_ref[...] = held[mine, 1, :, cols]

    def drain(zp, _):
        g_x(zp, d).wait_send()
        g_y(zp, d).wait_send()
        g_xh(zp, dy).wait_send()
        g_yh(zp, dx).wait_send()
        b_xh(zp).wait_send()
        b_yh(zp).wait_send()
        b_x(zp).wait_send()
        b_y(zp).wait_send()

        @pl.when(jnp.logical_and(zp <= z, has_up))
        def _():
            g_up(zp).wait_send()

        @pl.when(jnp.logical_and(zp >= z, has_down))
        def _():
            g_down(zp).wait_send()

        @pl.when(zp > z)
        def _():
            b_up(zp).wait_send()

        @pl.when(zp < z)
        def _():
            b_down(zp).wait_send()

        def chips(c, _):
            g_core(zp * 4 + c).wait_send()
            b_core(zp * 4 + c).wait_send()
            return 0

        lax.fori_loop(0, 4, chips, 0)
        return 0

    lax.fori_loop(0, layers, drain, 0)


def fused(tokens, node_choice, local_pick, gate_scores, placement, w_gate, w_up, w_down):
    tok, width = tokens.shape
    hidden = w_gate.shape[2]
    layers = lax.axis_size("node") // 2
    chips = layers * 4
    place = jnp.pad(placement, (0, 128 - placement.shape[0]), constant_values=-1)[None, :]
    vmem = pl.BlockSpec(memory_space=pltpu.VMEM)
    any_space = pl.BlockSpec(memory_space=pl.ANY)
    bf16 = jnp.bfloat16
    dma = pltpu.SemaphoreType.DMA
    return pl.pallas_call(
        functools.partial(fused_kernel, layers),
        out_shape=jax.ShapeDtypeStruct((tok, width), bf16),
        in_specs=[vmem] * 5 + [any_space] * 3,
        out_specs=vmem,
        scratch_shapes=[
            pltpu.VMEM((chips, 2, tok, width + 128), bf16),
            pltpu.VMEM((chips, tok, width), bf16),
            pltpu.VMEM((chips, tok, width), bf16),
            pltpu.VMEM((layers, tok // 2, width), bf16),
            pltpu.VMEM((layers, tok // 2, width), bf16),
            pltpu.VMEM((layers, tok, width), bf16),
            pltpu.VMEM((layers, tok, width), bf16),
            pltpu.VMEM((layers, tok, width), bf16),
            pltpu.VMEM((layers, tok, width), bf16),
            pltpu.VMEM((width, hidden), bf16),
            pltpu.VMEM((width, hidden), bf16),
            pltpu.VMEM((hidden, width), bf16),
            pltpu.VMEM((2 * tok, hidden), bf16),
            dma((chips,)),
            dma((chips,)),
            dma((chips,)),
            dma((chips,)),
            dma((12, layers)),
            dma((12, layers)),
            dma((3,)),
        ],
        compiler_params=pltpu.CompilerParams(
            collective_id=0, has_side_effects=True, vmem_limit_bytes=61 * 2**20
        ),
        cost_estimate=pl.CostEstimate(
            flops=6 * 2 * chips * tok * width * hidden,
            bytes_accessed=6 * width * hidden,
            transcendentals=2 * chips * tok * hidden,
        ),
        name="fused_experts",
    )(
        tokens,
        node_choice,
        local_pick.reshape(tok, -1),
        gate_scores,
        place,
        w_gate,
        w_up,
        w_down,
    )


def solution(mesh):
    small = mesh.shape["node"] == 8 and mesh.shape["dev"] == 4
    return jax.shard_map(
        fused if small else local,
        mesh=mesh,
        in_specs=(
            P(("group", "node", "dev"), None),
            P(("group", "node", "dev"), None),
            P(("group", "node", "dev"), None, None),
            P(("group", "node", "dev"), None),
            P(),
            P(("node", "dev"), None, None),
            P(("node", "dev"), None, None),
            P(("node", "dev"), None, None),
        ),
        out_specs=P(("group", "node", "dev"), None),
        check_vma=False,
    )
```

```python
import functools

import jax
import jax.numpy as jnp
from jax import lax
from jax.experimental import pallas as pl
from jax.experimental.pallas import tpu as pltpu
from jax.sharding import PartitionSpec as P

MESH = pl.DeviceIdType.MESH
ROWS = 16


def expert_terms(slot_rows, slot_gates, gate_matrix, up_matrix, down_matrix):
    row_total = slot_rows.shape[0]
    width = slot_rows.shape[1]
    live_mask = slot_gates > 0
    live_int = live_mask.astype(jnp.int32)
    live_count = jnp.sum(live_int)
    live_before = jnp.cumsum(live_int) - live_int
    spare_before = jnp.arange(row_total, dtype=jnp.int32) - live_before
    position = jnp.where(live_mask, live_before, live_count + spare_before)
    block_rows = min(512, row_total)
    padded_rows = -(-row_total // block_rows) * block_rows
    packed = jnp.zeros((padded_rows, width), jnp.bfloat16).at[position].set(slot_rows)
    outputs = jnp.zeros((padded_rows, down_matrix.shape[1]), jnp.bfloat16)

    def one_block(block_index, outputs):
        first_row = block_index * block_rows
        row_block = lax.dynamic_slice_in_dim(packed, first_row, block_rows, 0)
        gate_part = jnp.dot(row_block, gate_matrix, preferred_element_type=jnp.float32)
        up_part = jnp.dot(row_block, up_matrix, preferred_element_type=jnp.float32)
        hidden = (jax.nn.silu(gate_part) * up_part).astype(jnp.bfloat16)
        result = jnp.dot(hidden, down_matrix, preferred_element_type=jnp.float32).astype(
            jnp.bfloat16
        )
        return lax.dynamic_update_slice_in_dim(outputs, result, first_row, 0)

    block_count = (live_count + block_rows - 1) // block_rows
    outputs = lax.fori_loop(0, block_count, one_block, outputs)
    restored = outputs[position]
    return (slot_gates.astype(jnp.float32)[:, None] * restored.astype(jnp.float32)).astype(
        jnp.bfloat16
    )


def arrival_ranks(targets, target_count):
    onehot = (targets[:, None] == jnp.arange(target_count, dtype=jnp.int32)).astype(jnp.int32)
    return jnp.sum(jnp.cumsum(onehot, axis=0) * onehot, axis=-1) - 1


def local(tokens, node_choice, local_pick, gate_scores, placement, w_gate, w_up, w_down):
    tok_count = tokens.shape[0]
    width = tokens.shape[1]
    groups_each = node_choice.shape[1]
    pair_each = local_pick.shape[2]
    node_count = lax.axis_size("node")
    dev_count = lax.axis_size("dev")
    expert_total = placement.shape[0]
    capacity = min(tok_count, max(2, 3 * tok_count * groups_each // (2 * node_count)))
    gate_matrix = w_gate[0]
    up_matrix = w_up[0]
    down_matrix = w_down[0]
    expert_ids = node_choice[:, :, None] * dev_count + local_pick
    matches = expert_ids[..., None] == jnp.arange(expert_total, dtype=jnp.int32)
    slot_ids = jnp.sum(jnp.where(matches, placement, 0), axis=-1)
    raw_scores = jnp.sum(jnp.where(matches, gate_scores[:, None, None, :], 0.0), axis=-1)
    gate_values = (raw_scores / jnp.sum(raw_scores, axis=(1, 2), keepdims=True)).astype(
        jnp.bfloat16
    )
    flat_slots = slot_ids.reshape(-1)
    slot_ranks = arrival_ranks(flat_slots, expert_total)
    target = flat_slots * capacity + slot_ranks
    pair_rows = jnp.broadcast_to(
        tokens[:, None, None, :], (tok_count, groups_each, pair_each, width)
    ).reshape(-1, width)
    send_rows = jnp.zeros((expert_total * capacity, width), jnp.bfloat16).at[target].set(pair_rows)
    send_gates = (
        jnp.zeros((expert_total * capacity,), jnp.bfloat16).at[target].set(gate_values.reshape(-1))
    )
    recv_rows, recv_gates = (
        lax.all_to_all(
            send_rows.reshape(expert_total, capacity, width),
            ("node", "dev"),
            split_axis=0,
            concat_axis=0,
            tiled=True,
        ),
        lax.all_to_all(
            send_gates.reshape(expert_total, capacity),
            ("node", "dev"),
            split_axis=0,
            concat_axis=0,
            tiled=True,
        ),
    )
    weighted = expert_terms(
        recv_rows.reshape(-1, width), recv_gates.reshape(-1), gate_matrix, up_matrix, down_matrix
    )
    returned = lax.all_to_all(
        weighted.reshape(expert_total, capacity, width),
        ("node", "dev"),
        split_axis=0,
        concat_axis=0,
        tiled=True,
    )
    pair_terms = returned.reshape(-1, width)[target].reshape(
        tok_count, groups_each, pair_each, width
    )
    node_part = jnp.sum(pair_terms.astype(jnp.float32), axis=2).astype(jnp.bfloat16)
    return jnp.sum(node_part.astype(jnp.float32), axis=1).astype(jnp.bfloat16)


def fused_kernel(layers, tok_ref, node_ref, pick_ref, score_ref, place_ref, wg_hbm, wu_hbm, wd_hbm,
                 out_ref, held, spare, from_core, half_x, half_y, whole_x, whole_y, from_z, from_layer,
                 wg, wu, wd, hid, core_s, core_r, back_s, back_r, ax_s, ax_r, load_s):
    tok, width = tok_ref.shape
    half = tok // 2
    n = lax.axis_index("node")
    d = lax.axis_index("dev")
    z, k = n // 2, n % 2
    x, y = d % 2, d // 2
    dx = y * 2 + (1 - x)
    dy = (1 - y) * 2 + x
    dd = (1 - y) * 2 + (1 - x)
    mate = {"node": z * 2 + 1 - k, "dev": d}
    to_x = {"node": n, "dev": dx}
    to_y = {"node": n, "dev": dy}
    up = {"node": n + 2, "dev": d}
    down = {"node": n - 2, "dev": d}
    to_z = {"node": (z + 1 - 2 * (z % 2)) * 2 + k, "dev": d}
    has_up, has_down = z < layers - 1, z > 0
    middle = ((z + 1) // 2) % 2

    def near(j):
        j = j + middle * (j // 2) * (5 - 2 * j)
        return ((z // 2 + j // 2) % 2) * 2 + (z + j) % 2

    loads = [
        pltpu.make_async_copy(src.at[0], dst, load_s.at[i])
        for i, (src, dst) in enumerate(((wg_hbm, wg), (wu_hbm, wu), (wd_hbm, wd)))
    ]
    for load in loads:
        load.start()

    experts = score_ref.shape[0]
    row = lax.broadcasted_iota(jnp.int32, (experts, tok), 0)
    hit = jnp.zeros((experts, tok), jnp.float32)
    for g in range(pick_ref.shape[0]):
        for p in range(pick_ref.shape[1]):
            expert = node_ref[g : g + 1, :] * 4 + pick_ref[g, p : p + 1, :]
            hit = jnp.where(row == expert, 1.0, hit)
    raw = hit * score_ref[...]
    gates = raw / jnp.sum(raw, axis=0, keepdims=True)
    gates = jnp.concatenate([gates, jnp.zeros((128 - experts, tok), jnp.float32)], axis=0)
    mine = z * 4 + d
    held[mine, 0, :, pl.ds(0, width)] = tok_ref[...]
    held[mine, 0, :, pl.ds(width, 128)] = gates.T.astype(jnp.bfloat16)

    barrier = pltpu.get_barrier_semaphore()
    layer_of = [{"node": ((z + i) % layers) * 2 + k, "dev": d} for i in range(1, layers)]
    for other in [mate, to_x, to_y] + layer_of:
        pl.semaphore_signal(barrier, inc=1, device_id=other, device_id_type=MESH)
    pl.semaphore_wait(barrier, layers + 2)

    def remote(src, dst, send, recv, to):
        return pltpu.make_async_remote_copy(
            src_ref=src, dst_ref=dst, send_sem=send, recv_sem=recv, device_id=to,
            device_id_type=MESH,
        )

    def along(kind, zp, src, dst, to):
        return remote(src, dst, ax_s.at[kind, zp], ax_r.at[kind, zp], to)

    lo, hi = pl.ds(0, half), pl.ds(half, half)
    cols = pl.ds(0, width)

    def g_up(zp):
        return along(0, zp, held.at[zp * 4 + d, 0], held.at[zp * 4 + d, 0], up)

    def g_down(zp):
        return along(1, zp, held.at[zp * 4 + d, 0], held.at[zp * 4 + d, 0], down)

    def g_x(zp, dev):
        return along(2, zp, held.at[zp * 4 + dev, 0], held.at[zp * 4 + dev, 0], to_x)

    def g_y(zp, dev):
        return along(3, zp, held.at[zp * 4 + dev, 0], held.at[zp * 4 + dev, 0], to_y)

    def g_xh(zp, dev):
        part = held.at[zp * 4 + dev, 0, hi]
        return along(4, zp, part, part, to_x)

    def g_yh(zp, dev):
        part = held.at[zp * 4 + dev, 0, lo]
        return along(5, zp, part, part, to_y)

    def g_z(zp):
        return along(6, zp, held.at[zp * 4 + dd, 0], held.at[zp * 4 + dd, 0], to_z)

    def g_core(chip):
        return remote(held.at[chip, 0], held.at[chip, 1], core_s.at[chip], core_r.at[chip], mate)

    def b_core(chip):
        return remote(spare.at[chip], from_core.at[chip], back_s.at[chip], back_r.at[chip], mate)

    def b_xh(zp):
        return along(7, zp, held.at[zp * 4 + dd, 1, lo, cols], half_x.at[zp], to_x)

    def b_yh(zp):
        return along(8, zp, held.at[zp * 4 + dd, 1, hi, cols], half_y.at[zp], to_y)

    def b_x(zp):
        return along(9, zp, held.at[zp * 4 + dx, 1, :, cols], whole_x.at[zp], to_x)

    def b_y(zp):
        return along(10, zp, held.at[zp * 4 + dy, 1, :, cols], whole_y.at[zp], to_y)

    def b_z(zp):
        return along(11, zp, held.at[zp * 4 + dd, 1, :, cols], from_z.at[zp], to_z)

    def b_layer(zp, source):
        return remote(
            held.at[zp * 4 + d, 1, :, cols], from_layer.at[source], ax_s.at[12, zp],
            ax_r.at[12, source], {"node": zp * 2 + k, "dev": d},
        )

    here = (place_ref[...] == n * 4 + d).astype(jnp.float32)
    mask = jnp.concatenate([here, jnp.zeros((1, 128 - experts), jnp.float32)], axis=1)

    def experts_of(chip):
        def first(i, _):
            at = pl.ds(pl.multiple_of(i * 256, 256), 256)
            rows = held[chip, :, :, cols].reshape(2 * tok, width)
            a = jnp.dot(rows, wg[:, at], preferred_element_type=jnp.float32)
            b = jnp.dot(rows, wu[:, at], preferred_element_type=jnp.float32)
            hid[:, at] = (a / (1.0 + jnp.exp(-a)) * b).astype(jnp.bfloat16)
            return 0

        lax.fori_loop(0, wg.shape[1] // 256, first, 0, unroll=True)
        weights = held[chip, :, :, pl.ds(width, 128)].reshape(2 * tok, 128).astype(jnp.float32)
        weight = jnp.sum(weights * mask, axis=1, keepdims=True)

        def second(i, _):
            at = pl.ds(pl.multiple_of(i * 256, 256), 256)
            got = jnp.dot(hid[...], wd[:, at], preferred_element_type=jnp.float32)
            term = (weight * got.astype(jnp.bfloat16).astype(jnp.float32)).astype(jnp.bfloat16)
            held[chip, 1, :, at] = term[:tok]
            spare[chip, :, at] = term[tok:]
            return 0

        lax.fori_loop(0, width // 256, second, 0, unroll=True)

    def listed(q, act):
        t, c = q // 5, q % 5
        j = t - (c + 1) // 2 - c // 4

        @pl.when(jnp.logical_and(j >= 0, j < layers))
        def _():
            zp = near(j)
            other = (zp + z) % 2

            @pl.when(jnp.logical_or(c < 3, c == 3 + other))
            def _():
                cx = (x + c % 2 + c // 4) % 2
                cy = (y + c // 2 - c // 4) % 2
                act(c, zp, zp * 4 + cy * 2 + cx)

    def arrive(c, zp, chip):
        @pl.when(c == 0)
        def _():
            @pl.when(zp < z)
            def _():
                g_up(zp).wait_recv()

            @pl.when(zp > z)
            def _():
                g_down(zp).wait_recv()

            @pl.when(jnp.logical_and(zp <= z, has_up))
            def _():
                g_up(zp).start()

            @pl.when(jnp.logical_and(zp >= z, has_down))
            def _():
                g_down(zp).start()

            g_x(zp, d).start()
            g_y(zp, d).start()

        @pl.when(c == 1)
        def _():
            g_x(zp, dx).wait_recv()

            @pl.when((zp + z) % 2 == 0)
            def _():
                g_yh(zp, dx).start()

        @pl.when(c == 2)
        def _():
            g_y(zp, dy).wait_recv()

            @pl.when((zp + z) % 2 == 0)
            def _():
                g_xh(zp, dy).start()

        @pl.when(c == 3)
        def _():
            g_xh(zp, dd).wait_recv()
            g_yh(zp, dd).wait_recv()
            g_z(zp).start()

        @pl.when(c == 4)
        def _():
            g_z(zp).wait_recv()

        g_core(chip).start()

    def work(c, zp, chip):
        g_core(chip).wait_recv()
        experts_of(chip)
        b_core(chip).start()

    def gather_step(q, _):
        listed(q, arrive)

        @pl.when(q == 0)
        def _():
            for load in loads:
                load.wait()

        @pl.when(q >= 1)
        def _():
            listed(q - 1, work)

        return 0

    lax.fori_loop(0, 5 * (layers + 3) + 1, gather_step, 0)

    def total(chip, count, extra):
        def rows(i, _):
            at = pl.ds(pl.multiple_of(i * ROWS, ROWS), ROWS)
            value = held[chip, 1, at, cols].astype(jnp.float32)
            value = value + from_core[chip, at, :].astype(jnp.float32)
            for ref, zp in extra:
                value = value + ref[zp, at, :].astype(jnp.float32)
            held[chip, 1, at, cols] = value.astype(jnp.bfloat16)
            return 0

        lax.fori_loop(0, count // ROWS, rows, 0)

    def more(chip, first, count, ref, zp):
        def rows(i, _):
            at = pl.ds(pl.multiple_of(i * ROWS, ROWS), ROWS)
            to = pl.ds(pl.multiple_of(first + i * ROWS, ROWS), ROWS)
            value = held[chip, 1, to, cols].astype(jnp.float32) + ref[zp, at, :].astype(jnp.float32)
            held[chip, 1, to, cols] = value.astype(jnp.bfloat16)
            return 0

        lax.fori_loop(0, count // ROWS, rows, 0)

    def back_step(u, _):
        @pl.when(u < layers)
        def _():
            zp = near(layers - 1 - u)
            chip = zp * 4 + dd

            @pl.when((zp + z) % 2 == 1)
            def _():
                b_core(chip).wait_recv()
                total(chip, tok, ())
                b_z(zp).start()

        @pl.when(jnp.logical_and(u >= 1, u < layers + 1))
        def _():
            zp = near(layers - u)
            chip = zp * 4 + dd

            @pl.when((zp + z) % 2 == 0)
            def _():
                b_core(chip).wait_recv()
                b_z(zp).wait_recv()
                total(chip, tok, ((from_z, zp),))
                b_xh(zp).start()
                b_yh(zp).start()

        @pl.when(jnp.logical_and(u >= 2, u < layers + 2))
        def _():
            zp = near(layers + 1 - u)
            b_core(zp * 4 + dx).wait_recv()
            total(zp * 4 + dx, tok, ())

            @pl.when((zp + z) % 2 == 0)
            def _():
                b_yh(zp).wait_recv()
                more(zp * 4 + dx, half, half, half_y, zp)

            b_x(zp).start()
            b_core(zp * 4 + dy).wait_recv()
            total(zp * 4 + dy, tok, ())

            @pl.when((zp + z) % 2 == 0)
            def _():
                b_xh(zp).wait_recv()
                more(zp * 4 + dy, 0, half, half_x, zp)

            b_y(zp).start()

        @pl.when(u >= 3)
        def _():
            zp = near(layers + 2 - u)
            chip = zp * 4 + d
            b_core(chip).wait_recv()
            b_x(zp).wait_recv()
            b_y(zp).wait_recv()

            @pl.when(u < layers + 2)
            def _():
                total(chip, tok, ((whole_x, zp), (whole_y, zp)))
                b_layer(zp, z).start()

            @pl.when(u == layers + 2)
            def _():
                sources = [near(i) for i in range(1, layers)]
                for source in sources:
                    b_layer(source, source).wait_recv()
                total(
                    chip, tok,
                    [(whole_x, zp), (whole_y, zp)] + [(from_layer, source) for source in sources],
                )

        return 0

    lax.fori_loop(0, layers + 3, back_step, 0)
    out_ref[...] = held[mine, 1, :, cols]

    def drain(zp, _):
        g_x(zp, d).wait_send()
        g_y(zp, d).wait_send()
        b_x(zp).wait_send()
        b_y(zp).wait_send()

        @pl.when((zp + z) % 2 == 0)
        def _():
            g_xh(zp, dy).wait_send()
            g_yh(zp, dx).wait_send()
            g_z(zp).wait_send()
            b_xh(zp).wait_send()
            b_yh(zp).wait_send()

        @pl.when((zp + z) % 2 == 1)
        def _():
            b_z(zp).wait_send()

        @pl.when(zp < z)
        def _():
            b_layer(zp, z).wait_send()

        @pl.when(zp > z)
        def _():
            b_layer(zp, z).wait_send()

        @pl.when(jnp.logical_and(zp <= z, has_up))
        def _():
            g_up(zp).wait_send()

        @pl.when(jnp.logical_and(zp >= z, has_down))
        def _():
            g_down(zp).wait_send()

        def chips(c, _):
            g_core(zp * 4 + c).wait_send()
            b_core(zp * 4 + c).wait_send()
            return 0

        lax.fori_loop(0, 4, chips, 0)
        return 0

    lax.fori_loop(0, layers, drain, 0)


def fused(tokens, node_choice, local_pick, gate_scores, placement, w_gate, w_up, w_down):
    tok, width = tokens.shape
    hidden = w_gate.shape[2]
    layers = lax.axis_size("node") // 2
    chips = layers * 4
    vmem = pl.BlockSpec(memory_space=pltpu.VMEM)
    any_space = pl.BlockSpec(memory_space=pl.ANY)
    bf16 = jnp.bfloat16
    dma = pltpu.SemaphoreType.DMA
    return pl.pallas_call(
        functools.partial(fused_kernel, layers),
        out_shape=jax.ShapeDtypeStruct((tok, width), bf16),
        in_specs=[vmem] * 5 + [any_space] * 3,
        out_specs=vmem,
        scratch_shapes=[
            pltpu.VMEM((chips, 2, tok, width + 128), bf16),
            pltpu.VMEM((chips, tok, width), bf16),
            pltpu.VMEM((chips, tok, width), bf16),
            pltpu.VMEM((layers, tok // 2, width), bf16),
            pltpu.VMEM((layers, tok // 2, width), bf16),
            pltpu.VMEM((layers, tok, width), bf16),
            pltpu.VMEM((layers, tok, width), bf16),
            pltpu.VMEM((layers, tok, width), bf16),
            pltpu.VMEM((layers, tok, width), bf16),
            pltpu.VMEM((width, hidden), bf16),
            pltpu.VMEM((width, hidden), bf16),
            pltpu.VMEM((hidden, width), bf16),
            pltpu.VMEM((2 * tok, hidden), bf16),
            dma((chips,)),
            dma((chips,)),
            dma((chips,)),
            dma((chips,)),
            dma((13, layers)),
            dma((13, layers)),
            dma((3,)),
        ],
        compiler_params=pltpu.CompilerParams(
            collective_id=0, has_side_effects=True, vmem_limit_bytes=61 * 2**20
        ),
        cost_estimate=pl.CostEstimate(
            flops=6 * 2 * chips * tok * width * hidden,
            bytes_accessed=6 * width * hidden,
            transcendentals=2 * chips * tok * hidden,
        ),
        name="fused_experts",
    )(
        tokens,
        node_choice.T,
        local_pick.transpose(1, 2, 0),
        gate_scores.T,
        placement[None, :],
        w_gate,
        w_up,
        w_down,
    )


def solution(mesh):
    small = mesh.shape["node"] == 8 and mesh.shape["dev"] == 4
    return jax.shard_map(
        fused if small else local,
        mesh=mesh,
        in_specs=(
            P(("group", "node", "dev"), None),
            P(("group", "node", "dev"), None),
            P(("group", "node", "dev"), None, None),
            P(("group", "node", "dev"), None),
            P(),
            P(("node", "dev"), None, None),
            P(("node", "dev"), None, None),
            P(("node", "dev"), None, None),
        ),
        out_specs=P(("group", "node", "dev"), None),
        check_vma=False,
    )
```

```python
import functools

import jax
import jax.numpy as jnp
from jax import lax
from jax.experimental import pallas as pl
from jax.experimental.pallas import tpu as pltpu
from jax.sharding import PartitionSpec as P

MESH = pl.DeviceIdType.MESH
ROWS = 16


def expert_terms(slot_rows, slot_gates, gate_matrix, up_matrix, down_matrix):
    row_total = slot_rows.shape[0]
    width = slot_rows.shape[1]
    live_mask = slot_gates > 0
    live_int = live_mask.astype(jnp.int32)
    live_count = jnp.sum(live_int)
    live_before = jnp.cumsum(live_int) - live_int
    spare_before = jnp.arange(row_total, dtype=jnp.int32) - live_before
    position = jnp.where(live_mask, live_before, live_count + spare_before)
    block_rows = min(512, row_total)
    padded_rows = -(-row_total // block_rows) * block_rows
    packed = jnp.zeros((padded_rows, width), jnp.bfloat16).at[position].set(slot_rows)
    outputs = jnp.zeros((padded_rows, down_matrix.shape[1]), jnp.bfloat16)

    def one_block(block_index, outputs):
        first_row = block_index * block_rows
        row_block = lax.dynamic_slice_in_dim(packed, first_row, block_rows, 0)
        gate_part = jnp.dot(row_block, gate_matrix, preferred_element_type=jnp.float32)
        up_part = jnp.dot(row_block, up_matrix, preferred_element_type=jnp.float32)
        hidden = (jax.nn.silu(gate_part) * up_part).astype(jnp.bfloat16)
        result = jnp.dot(hidden, down_matrix, preferred_element_type=jnp.float32).astype(
            jnp.bfloat16
        )
        return lax.dynamic_update_slice_in_dim(outputs, result, first_row, 0)

    block_count = (live_count + block_rows - 1) // block_rows
    outputs = lax.fori_loop(0, block_count, one_block, outputs)
    restored = outputs[position]
    return (slot_gates.astype(jnp.float32)[:, None] * restored.astype(jnp.float32)).astype(
        jnp.bfloat16
    )


def arrival_ranks(targets, target_count):
    onehot = (targets[:, None] == jnp.arange(target_count, dtype=jnp.int32)).astype(jnp.int32)
    return jnp.sum(jnp.cumsum(onehot, axis=0) * onehot, axis=-1) - 1


def local(tokens, node_choice, local_pick, gate_scores, placement, w_gate, w_up, w_down):
    tok_count = tokens.shape[0]
    width = tokens.shape[1]
    groups_each = node_choice.shape[1]
    pair_each = local_pick.shape[2]
    node_count = lax.axis_size("node")
    dev_count = lax.axis_size("dev")
    expert_total = placement.shape[0]
    capacity = min(tok_count, max(2, 3 * tok_count * groups_each // (2 * node_count)))
    gate_matrix = w_gate[0]
    up_matrix = w_up[0]
    down_matrix = w_down[0]
    expert_ids = node_choice[:, :, None] * dev_count + local_pick
    matches = expert_ids[..., None] == jnp.arange(expert_total, dtype=jnp.int32)
    slot_ids = jnp.sum(jnp.where(matches, placement, 0), axis=-1)
    raw_scores = jnp.sum(jnp.where(matches, gate_scores[:, None, None, :], 0.0), axis=-1)
    gate_values = (raw_scores / jnp.sum(raw_scores, axis=(1, 2), keepdims=True)).astype(
        jnp.bfloat16
    )
    flat_slots = slot_ids.reshape(-1)
    slot_ranks = arrival_ranks(flat_slots, expert_total)
    target = flat_slots * capacity + slot_ranks
    pair_rows = jnp.broadcast_to(
        tokens[:, None, None, :], (tok_count, groups_each, pair_each, width)
    ).reshape(-1, width)
    send_rows = jnp.zeros((expert_total * capacity, width), jnp.bfloat16).at[target].set(pair_rows)
    send_gates = (
        jnp.zeros((expert_total * capacity,), jnp.bfloat16).at[target].set(gate_values.reshape(-1))
    )
    recv_rows, recv_gates = (
        lax.all_to_all(
            send_rows.reshape(expert_total, capacity, width),
            ("node", "dev"),
            split_axis=0,
            concat_axis=0,
            tiled=True,
        ),
        lax.all_to_all(
            send_gates.reshape(expert_total, capacity),
            ("node", "dev"),
            split_axis=0,
            concat_axis=0,
            tiled=True,
        ),
    )
    weighted = expert_terms(
        recv_rows.reshape(-1, width), recv_gates.reshape(-1), gate_matrix, up_matrix, down_matrix
    )
    returned = lax.all_to_all(
        weighted.reshape(expert_total, capacity, width),
        ("node", "dev"),
        split_axis=0,
        concat_axis=0,
        tiled=True,
    )
    pair_terms = returned.reshape(-1, width)[target].reshape(
        tok_count, groups_each, pair_each, width
    )
    node_part = jnp.sum(pair_terms.astype(jnp.float32), axis=2).astype(jnp.bfloat16)
    return jnp.sum(node_part.astype(jnp.float32), axis=1).astype(jnp.bfloat16)


def fused_kernel(layers, tok_ref, node_ref, pick_ref, score_ref, place_ref, wg_hbm, wu_hbm, wd_hbm,
                 out_ref, held, spare, from_core, half_x, half_y, whole_x, whole_y, from_layer,
                 wg, wu, wd, hid, core_s, core_r, back_s, back_r, ax_s, ax_r, load_s):
    tok, width = tok_ref.shape
    half = tok // 2
    n = lax.axis_index("node")
    d = lax.axis_index("dev")
    z, k = n // 2, n % 2
    x, y = d % 2, d // 2
    dx = y * 2 + (1 - x)
    dy = (1 - y) * 2 + x
    dd = (1 - y) * 2 + (1 - x)
    mate = {"node": z * 2 + 1 - k, "dev": d}
    to_x = {"node": n, "dev": dx}
    to_y = {"node": n, "dev": dy}
    up = {"node": n + 2, "dev": d}
    down = {"node": n - 2, "dev": d}
    has_up, has_down = z < layers - 1, z > 0
    middle = ((z + 1) // 2) % 2

    def near(j):
        j = j + middle * (j // 2) * (5 - 2 * j)
        return ((z // 2 + j // 2) % 2) * 2 + (z + j) % 2

    loads = [
        pltpu.make_async_copy(src.at[0], dst, load_s.at[i])
        for i, (src, dst) in enumerate(((wg_hbm, wg), (wu_hbm, wu), (wd_hbm, wd)))
    ]
    for load in loads:
        load.start()

    experts = score_ref.shape[0]
    row = lax.broadcasted_iota(jnp.int32, (experts, tok), 0)
    hit = jnp.zeros((experts, tok), jnp.float32)
    for g in range(pick_ref.shape[0]):
        for p in range(pick_ref.shape[1]):
            expert = node_ref[g : g + 1, :] * 4 + pick_ref[g, p : p + 1, :]
            hit = jnp.where(row == expert, 1.0, hit)
    raw = hit * score_ref[...]
    gates = raw / jnp.sum(raw, axis=0, keepdims=True)
    gates = jnp.concatenate([gates, jnp.zeros((128 - experts, tok), jnp.float32)], axis=0)
    mine = z * 4 + d
    held[mine, 0, :, pl.ds(0, width)] = tok_ref[...]
    held[mine, 0, :, pl.ds(width, 128)] = gates.T.astype(jnp.bfloat16)

    barrier = pltpu.get_barrier_semaphore()
    layer_of = [{"node": ((z + i) % layers) * 2 + k, "dev": d} for i in range(1, layers)]
    for other in [mate, to_x, to_y] + layer_of:
        pl.semaphore_signal(barrier, inc=1, device_id=other, device_id_type=MESH)
    pl.semaphore_wait(barrier, layers + 2)

    def remote(src, dst, send, recv, to):
        return pltpu.make_async_remote_copy(
            src_ref=src, dst_ref=dst, send_sem=send, recv_sem=recv, device_id=to,
            device_id_type=MESH,
        )

    def along(kind, zp, src, dst, to):
        return remote(src, dst, ax_s.at[kind, zp], ax_r.at[kind, zp], to)

    lo, hi = pl.ds(0, half), pl.ds(half, half)
    cols = pl.ds(0, width)

    def g_up(zp):
        return along(0, zp, held.at[zp * 4 + d, 0], held.at[zp * 4 + d, 0], up)

    def g_down(zp):
        return along(1, zp, held.at[zp * 4 + d, 0], held.at[zp * 4 + d, 0], down)

    def g_x(zp, dev):
        return along(2, zp, held.at[zp * 4 + dev, 0], held.at[zp * 4 + dev, 0], to_x)

    def g_y(zp, dev):
        return along(3, zp, held.at[zp * 4 + dev, 0], held.at[zp * 4 + dev, 0], to_y)

    def g_xh(zp, dev):
        part = held.at[zp * 4 + dev, 0, hi]
        return along(4, zp, part, part, to_x)

    def g_yh(zp, dev):
        part = held.at[zp * 4 + dev, 0, lo]
        return along(5, zp, part, part, to_y)

    def g_core(chip):
        return remote(held.at[chip, 0], held.at[chip, 1], core_s.at[chip], core_r.at[chip], mate)

    def b_core(chip):
        return remote(spare.at[chip], from_core.at[chip], back_s.at[chip], back_r.at[chip], mate)

    def b_xh(zp):
        return along(7, zp, held.at[zp * 4 + dd, 1, lo, cols], half_x.at[zp], to_x)

    def b_yh(zp):
        return along(8, zp, held.at[zp * 4 + dd, 1, hi, cols], half_y.at[zp], to_y)

    def b_x(zp):
        return along(9, zp, held.at[zp * 4 + dx, 1, :, cols], whole_x.at[zp], to_x)

    def b_y(zp):
        return along(10, zp, held.at[zp * 4 + dy, 1, :, cols], whole_y.at[zp], to_y)

    def b_layer(zp, source):
        return remote(
            held.at[zp * 4 + d, 1, :, cols], from_layer.at[source], ax_s.at[12, zp],
            ax_r.at[12, source], {"node": zp * 2 + k, "dev": d},
        )

    here = (place_ref[...] == n * 4 + d).astype(jnp.float32)
    mask = jnp.concatenate([here, jnp.zeros((1, 128 - experts), jnp.float32)], axis=1)

    def experts_of(chip):
        def first(i, _):
            at = pl.ds(pl.multiple_of(i * 256, 256), 256)
            rows = held[chip, :, :, cols].reshape(2 * tok, width)
            a = jnp.dot(rows, wg[:, at], preferred_element_type=jnp.float32)
            b = jnp.dot(rows, wu[:, at], preferred_element_type=jnp.float32)
            hid[:, at] = (a / (1.0 + jnp.exp(-a)) * b).astype(jnp.bfloat16)
            return 0

        lax.fori_loop(0, wg.shape[1] // 256, first, 0, unroll=True)
        weights = held[chip, :, :, pl.ds(width, 128)].reshape(2 * tok, 128).astype(jnp.float32)
        weight = jnp.sum(weights * mask, axis=1, keepdims=True)

        def second(i, _):
            at = pl.ds(pl.multiple_of(i * 256, 256), 256)
            got = jnp.dot(hid[...], wd[:, at], preferred_element_type=jnp.float32)
            term = (weight * got.astype(jnp.bfloat16).astype(jnp.float32)).astype(jnp.bfloat16)
            held[chip, 1, :, at] = term[:tok]
            spare[chip, :, at] = term[tok:]
            return 0

        lax.fori_loop(0, width // 256, second, 0, unroll=True)

    def listed(q, act):
        t, c = q // 4, q % 4
        j = t - (c + 1) // 2

        @pl.when(jnp.logical_and(j >= 0, j < layers))
        def _():
            zp = near(j)
            act(c, zp, zp * 4 + (y + c // 2) % 2 * 2 + (x + c) % 2)

    def arrive(c, zp, chip):
        @pl.when(c == 0)
        def _():
            @pl.when(zp < z)
            def _():
                g_up(zp).wait_recv()

            @pl.when(zp > z)
            def _():
                g_down(zp).wait_recv()

            @pl.when(jnp.logical_and(zp <= z, has_up))
            def _():
                g_up(zp).start()

            @pl.when(jnp.logical_and(zp >= z, has_down))
            def _():
                g_down(zp).start()

            g_x(zp, d).start()
            g_y(zp, d).start()

        @pl.when(c == 1)
        def _():
            g_x(zp, dx).wait_recv()

            g_yh(zp, dx).start()

        @pl.when(c == 2)
        def _():
            g_y(zp, dy).wait_recv()

            g_xh(zp, dy).start()

        @pl.when(c == 3)
        def _():
            g_xh(zp, dd).wait_recv()
            g_yh(zp, dd).wait_recv()

        g_core(chip).start()

    def work(c, zp, chip):
        g_core(chip).wait_recv()
        experts_of(chip)
        b_core(chip).start()

    def gather_step(q, _):
        listed(q, arrive)

        @pl.when(q == 0)
        def _():
            for load in loads:
                load.wait()

        @pl.when(q >= 1)
        def _():
            listed(q - 1, work)

        return 0

    lax.fori_loop(0, 4 * (layers + 2) + 1, gather_step, 0)

    def total(chip, count, extra):
        def rows(i, _):
            at = pl.ds(pl.multiple_of(i * ROWS, ROWS), ROWS)
            value = held[chip, 1, at, cols].astype(jnp.float32)
            value = value + from_core[chip, at, :].astype(jnp.float32)
            for ref, zp in extra:
                value = value + ref[zp, at, :].astype(jnp.float32)
            held[chip, 1, at, cols] = value.astype(jnp.bfloat16)
            return 0

        lax.fori_loop(0, count // ROWS, rows, 0)

    def more(chip, first, count, ref, zp):
        def rows(i, _):
            at = pl.ds(pl.multiple_of(i * ROWS, ROWS), ROWS)
            to = pl.ds(pl.multiple_of(first + i * ROWS, ROWS), ROWS)
            value = held[chip, 1, to, cols].astype(jnp.float32) + ref[zp, at, :].astype(jnp.float32)
            held[chip, 1, to, cols] = value.astype(jnp.bfloat16)
            return 0

        lax.fori_loop(0, count // ROWS, rows, 0)

    def back_step(u, _):
        @pl.when(jnp.logical_and(u >= 1, u < layers + 1))
        def _():
            zp = near(layers - u)
            chip = zp * 4 + dd

            b_core(chip).wait_recv()
            total(chip, tok, ())
            b_xh(zp).start()
            b_yh(zp).start()

        @pl.when(jnp.logical_and(u >= 2, u < layers + 2))
        def _():
            zp = near(layers + 1 - u)
            b_core(zp * 4 + dx).wait_recv()
            total(zp * 4 + dx, tok, ())

            b_yh(zp).wait_recv()
            more(zp * 4 + dx, half, half, half_y, zp)

            b_x(zp).start()
            b_core(zp * 4 + dy).wait_recv()
            total(zp * 4 + dy, tok, ())

            b_xh(zp).wait_recv()
            more(zp * 4 + dy, 0, half, half_x, zp)

            b_y(zp).start()

        @pl.when(u >= 3)
        def _():
            zp = near(layers + 2 - u)
            chip = zp * 4 + d
            b_core(chip).wait_recv()
            b_x(zp).wait_recv()
            b_y(zp).wait_recv()

            @pl.when(u < layers + 2)
            def _():
                total(chip, tok, ((whole_x, zp), (whole_y, zp)))
                b_layer(zp, z).start()

            @pl.when(u == layers + 2)
            def _():
                sources = [near(i) for i in range(1, layers)]
                for source in sources:
                    b_layer(source, source).wait_recv()
                total(
                    chip, tok,
                    [(whole_x, zp), (whole_y, zp)] + [(from_layer, source) for source in sources],
                )

        return 0

    lax.fori_loop(1, layers + 3, back_step, 0)
    out_ref[...] = held[mine, 1, :, cols]

    def drain(zp, _):
        g_x(zp, d).wait_send()
        g_y(zp, d).wait_send()
        b_x(zp).wait_send()
        b_y(zp).wait_send()

        g_xh(zp, dy).wait_send()
        g_yh(zp, dx).wait_send()
        b_xh(zp).wait_send()
        b_yh(zp).wait_send()

        @pl.when(zp < z)
        def _():
            b_layer(zp, z).wait_send()

        @pl.when(zp > z)
        def _():
            b_layer(zp, z).wait_send()

        @pl.when(jnp.logical_and(zp <= z, has_up))
        def _():
            g_up(zp).wait_send()

        @pl.when(jnp.logical_and(zp >= z, has_down))
        def _():
            g_down(zp).wait_send()

        def chips(c, _):
            g_core(zp * 4 + c).wait_send()
            b_core(zp * 4 + c).wait_send()
            return 0

        lax.fori_loop(0, 4, chips, 0)
        return 0

    lax.fori_loop(0, layers, drain, 0)


def fused(tokens, node_choice, local_pick, gate_scores, placement, w_gate, w_up, w_down):
    tok, width = tokens.shape
    hidden = w_gate.shape[2]
    layers = lax.axis_size("node") // 2
    chips = layers * 4
    vmem = pl.BlockSpec(memory_space=pltpu.VMEM)
    any_space = pl.BlockSpec(memory_space=pl.ANY)
    bf16 = jnp.bfloat16
    dma = pltpu.SemaphoreType.DMA
    return pl.pallas_call(
        functools.partial(fused_kernel, layers),
        out_shape=jax.ShapeDtypeStruct((tok, width), bf16),
        in_specs=[vmem] * 5 + [any_space] * 3,
        out_specs=vmem,
        scratch_shapes=[
            pltpu.VMEM((chips, 2, tok, width + 128), bf16),
            pltpu.VMEM((chips, tok, width), bf16),
            pltpu.VMEM((chips, tok, width), bf16),
            pltpu.VMEM((layers, tok // 2, width), bf16),
            pltpu.VMEM((layers, tok // 2, width), bf16),
            pltpu.VMEM((layers, tok, width), bf16),
            pltpu.VMEM((layers, tok, width), bf16),
            pltpu.VMEM((layers, tok, width), bf16),
            pltpu.VMEM((width, hidden), bf16),
            pltpu.VMEM((width, hidden), bf16),
            pltpu.VMEM((hidden, width), bf16),
            pltpu.VMEM((2 * tok, hidden), bf16),
            dma((chips,)),
            dma((chips,)),
            dma((chips,)),
            dma((chips,)),
            dma((13, layers)),
            dma((13, layers)),
            dma((3,)),
        ],
        compiler_params=pltpu.CompilerParams(
            collective_id=0, has_side_effects=True, vmem_limit_bytes=61 * 2**20
        ),
        cost_estimate=pl.CostEstimate(
            flops=6 * 2 * chips * tok * width * hidden,
            bytes_accessed=6 * width * hidden,
            transcendentals=2 * chips * tok * hidden,
        ),
        name="fused_experts",
    )(
        tokens,
        node_choice.T,
        local_pick.transpose(1, 2, 0),
        gate_scores.T,
        placement[None, :],
        w_gate,
        w_up,
        w_down,
    )


def solution(mesh):
    small = mesh.shape["node"] == 8 and mesh.shape["dev"] == 4
    return jax.shard_map(
        fused if small else local,
        mesh=mesh,
        in_specs=(
            P(("group", "node", "dev"), None),
            P(("group", "node", "dev"), None),
            P(("group", "node", "dev"), None, None),
            P(("group", "node", "dev"), None),
            P(),
            P(("node", "dev"), None, None),
            P(("node", "dev"), None, None),
            P(("node", "dev"), None, None),
        ),
        out_specs=P(("group", "node", "dev"), None),
        check_vma=False,
    )
```
